32 devices in a mesh: head: 4 (over z), outer: 2 (over x), inner: 4 (over y, core).
Axes of the slice: x: 2, y: 2, z: 4, core: 2. Of those that a mesh axis runs over, the one named last changes fastest.
Arguments:
- tokens: bfloat16 [4096, 8192], P(('outer', 'inner')), may hold values from -16 to 16
- positions: int32 [4096], replicated, may hold values from 0 to 4095, as said below
- w_query: bfloat16 [8192, 4096], P(None, 'head'), as said below
- w_keyval: bfloat16 [8192, 1024], P(None, 'head'), as said below
Outputs:
- attended: bfloat16 [4096, 4096], P(('outer', 'inner'), 'head')
The draws below stay inside these ranges and needn't reach their ends.
Inputs may be any that keep to these rules, and one draw needn't show every extreme that they name: positions is a permutation of 0 to 4095 made of runs of 256 consecutive rising positions, each run starting at a multiple of 256. `w_query`: entries are of the order of the inverse square root of 8192. `w_keyval`: entries are of the order of the inverse square root of 8192.
All inputs are finite; a program needn't handle non-finite values.
Results may differ from the reference program's by a relative error of at most 0.011.
Values may be sent and summed in bfloat16 or wider, within the bound.
No kernel may reach another device: no remote copies, remote signals or barrier semaphores. Data moves between devices by JAX's collectives and lax.ppermute only.
A program may use at most 128 MiB of HBM per device.

```python
import jax
import jax.numpy as jnp
from jax import lax

D = 8192
HEADS = 32
KV_HEADS = 4
HEAD_DIM = 128
TOK_DEV = 512
SPAN = 256
SEQ = 4096


def shared_query(key):
    return jax.random.truncated_normal(key, -6.0, 6.0, (D, HEADS * HEAD_DIM), jnp.float32)


def draw_tokens(key, part):
    key = jax.random.fold_in(key, 11)
    first_key = jax.random.fold_in(key, 0)
    values = jax.random.truncated_normal(first_key, -6.0, 6.0, (SEQ, D), jnp.float32)
    return values.astype(jnp.bfloat16)


def draw_positions(key, part):
    key = jax.random.fold_in(key, 17)
    runs = SEQ // SPAN
    order = jax.random.permutation(key, runs).astype(jnp.int32)
    within = jnp.arange(SPAN, dtype=jnp.int32)
    return (order[:, None] * SPAN + within[None, :]).reshape(SEQ)


def draw_w_query(key, part):
    return (shared_query(key) * D ** (-0.5)).astype(jnp.bfloat16)


def draw_w_keyval(key, part):
    own_key = jax.random.fold_in(key, 23)
    fresh = jax.random.truncated_normal(own_key, -6.0, 6.0, (D, KV_HEADS, 2, HEAD_DIM), jnp.float32)
    return (fresh.reshape(D, KV_HEADS * 2 * HEAD_DIM) * D ** (-0.5)).astype(jnp.bfloat16)


def setup_inputs(seed: int = 0) -> dict:
    streams_of = jax.random.split(jax.random.key(seed), 5)
    tokens = draw_tokens(jax.random.fold_in(streams_of[4], 71), 0)
    positions = draw_positions(jax.random.fold_in(streams_of[4], 71), 0)
    w_query = draw_w_query(jax.random.fold_in(streams_of[4], 71), 0)
    w_keyval = draw_w_keyval(jax.random.fold_in(streams_of[4], 71), 0)
    return {"tokens": tokens, "positions": positions, "w_query": w_query, "w_keyval": w_keyval}


ROPE_BASE = 500000.0
NEG_FILL = -1e30


def rotary(values, where_pos):
    half = values.shape[-1] // 2
    freqs = jnp.power(ROPE_BASE, -(jnp.arange(half, dtype=jnp.float32) * 2.0) / values.shape[-1])
    angles = where_pos.astype(jnp.float32)[:, None] * freqs[None, :]
    cosine = jnp.cos(angles)[:, None, :]
    sine_part = jnp.sin(angles)[:, None, :]
    first_half = values[..., :half]
    second_half = values[..., half:]
    return jnp.concatenate([first_half * cosine - second_half * sine_part, second_half * cosine + first_half * sine_part], -1)


def reference(tokens, positions, w_query, w_keyval):
    seq = tokens.shape[0]
    group_size = HEADS // KV_HEADS
    blocks = seq // TOK_DEV
    projected = jnp.dot(tokens, w_query, preferred_element_type=jnp.float32).reshape(seq, HEADS, HEAD_DIM)
    queries = rotary(projected, positions).astype(jnp.bfloat16)
    keyval = jnp.dot(tokens, w_keyval, preferred_element_type=jnp.float32).reshape(seq, KV_HEADS, 2, HEAD_DIM)
    key_rows = rotary(keyval[:, :, 0], positions).astype(jnp.bfloat16)
    value_rows = keyval[:, :, 1].astype(jnp.bfloat16)
    head_queries = jnp.transpose(queries, (1, 0, 2)).reshape(HEADS, blocks, TOK_DEV, HEAD_DIM)
    block_positions = positions.reshape(blocks, TOK_DEV)

    def one_head(index):
        kv_index = index // group_size
        head_keys = jnp.take(key_rows, kv_index, axis=1).astype(jnp.float32)
        head_values = jnp.take(value_rows, kv_index, axis=1).astype(jnp.float32)
        own_queries = jnp.take(head_queries, index, axis=0)

        def one_block(items):
            block_q, block_pos = items
            scores = jnp.einsum("qd,kd->qk", block_q.astype(jnp.float32), head_keys) * (HEAD_DIM ** -0.5)
            allowed = positions[None, :] <= block_pos[:, None]
            scores = jnp.where(allowed, scores, NEG_FILL)
            top = jnp.max(scores, axis=-1, keepdims=True)
            weights = jnp.exp(scores - top)
            totals = jnp.sum(weights, axis=-1, keepdims=True)
            rounded = weights.astype(jnp.bfloat16).astype(jnp.float32)
            return jnp.einsum("qk,kd->qd", rounded, head_values) / totals

        return lax.map(one_block, (own_queries, block_positions))

    outputs = lax.map(one_head, jnp.arange(HEADS, dtype=jnp.int32))
    outputs = jnp.transpose(outputs, (1, 2, 0, 3)).reshape(seq, HEADS * HEAD_DIM)
    return outputs.astype(jnp.bfloat16)
```

```python
import functools
import math

import jax
import jax.numpy as jnp
import numpy as np
from jax import lax
from jax.experimental import pallas as pl
from jax.experimental.pallas import tpu as pltpu
from jax.sharding import PartitionSpec as P

HEAD_DIM = 128
HALF = HEAD_DIM // 2
SPAN = 256
ROPE_BASE = 500000.0
NEG_FILL = -1e30
LOG2_SCALE = math.log2(math.e) / math.sqrt(HEAD_DIM)
VMEM_LIMIT = 56 * 1024 * 1024
SEQ_AXES = ("outer", "inner")


def rotation_tables(runs):
    freqs = ROPE_BASE ** (-(np.arange(HALF, dtype=np.float64) * 2.0) / HEAD_DIM)
    freqs = np.concatenate([freqs, freqs])
    within = np.arange(SPAN, dtype=np.float64)[:, None] * freqs
    starts = (np.arange(runs, dtype=np.float64) * SPAN)[:, None] * freqs
    within = np.stack([np.cos(within), np.sin(within)]).astype(np.float32)
    starts = np.stack([np.cos(starts), np.sin(starts)], 1).astype(np.float32)
    return jnp.asarray(within), jnp.asarray(starts)


def run_rotation(within_ref, starts_ref, run):
    cos_in, sin_in = within_ref[0], within_ref[1]
    start = starts_ref[run]
    cos_at, sin_at = start[0:1], start[1:2]
    lane = lax.broadcasted_iota(jnp.int32, (1, HEAD_DIM), 1)
    sign = jnp.where(lane < HALF, -1.0, 1.0).astype(jnp.float32)
    cosine = cos_in * cos_at - sin_in * sin_at
    sine = (sin_in * cos_at + cos_in * sin_at) * sign
    return cosine, sine


def rotate(rows, cosine, sine):
    return rows * cosine + pltpu.roll(rows, HALF, 1) * sine


def own_run(pos_ref, index):
    row = lax.axis_index("outer") * lax.axis_size("inner") + lax.axis_index("inner")
    return pos_ref[row * (2 * SPAN) + index * SPAN] // SPAN


def projection_kernel(rotated, pos_ref, tokens_ref, w_ref, within_ref, starts_ref, out_ref, total):
    step = pl.program_id(0)
    product = jnp.dot(tokens_ref[...], w_ref[...], preferred_element_type=jnp.float32)

    @pl.when(step == 0)
    def _():
        total[...] = product

    @pl.when(step > 0)
    def _():
        total[...] += product

    @pl.when(step == pl.num_programs(0) - 1)
    def _():
        for part in range(out_ref.shape[0] // SPAN):
            rows = pl.ds(part * SPAN, SPAN)
            cosine, sine = run_rotation(within_ref, starts_ref, own_run(pos_ref, part))
            for column in range(out_ref.shape[1] // HEAD_DIM):
                cols = pl.ds(column * HEAD_DIM, HEAD_DIM)
                piece = total[rows, cols]
                if column < rotated:
                    piece = rotate(piece, cosine, sine)
                out_ref[rows, cols] = piece.astype(out_ref.dtype)


def project(tokens, weights, positions, tables, rotated, depth):
    rows, width = tokens.shape
    columns = weights.shape[1]
    within, starts = tables
    return pl.pallas_call(
        functools.partial(projection_kernel, rotated),
        grid=(width // depth,),
        in_specs=[
            pl.BlockSpec(memory_space=pltpu.SMEM),
            pl.BlockSpec((rows, depth), lambda k: (0, k)),
            pl.BlockSpec((depth, columns), lambda k: (k, 0)),
            pl.BlockSpec(within.shape, lambda k: (0, 0, 0)),
            pl.BlockSpec(starts.shape, lambda k: (0, 0, 0)),
        ],
        out_specs=pl.BlockSpec((rows, columns), lambda k: (0, 0)),
        out_shape=jax.ShapeDtypeStruct((rows, columns), jnp.bfloat16),
        scratch_shapes=[pltpu.VMEM((rows, columns), jnp.float32)],
        compiler_params=pltpu.CompilerParams(vmem_limit_bytes=VMEM_LIMIT),
        cost_estimate=pl.CostEstimate(
            flops=2 * rows * width * columns,
            bytes_accessed=2 * (rows * width + width * columns),
            transcendentals=0,
        ),
    )(positions, tokens, weights, within, starts)


def attention_kernel(masks, pos_ref, q_ref, kv_ref, out_ref, order, top_ref, total_ref):
    heads = q_ref.shape[1] // HEAD_DIM
    me = lax.axis_index("outer") * lax.axis_size("inner") + lax.axis_index("inner")
    causal = lax.broadcasted_iota(jnp.int32, (SPAN, SPAN), 1) <= lax.broadcasted_iota(
        jnp.int32, (SPAN, SPAN), 0
    )
    ones = jnp.ones((SPAN, HEAD_DIM), jnp.bfloat16)

    def visit(rows, slots, first):
        starts = [pl.multiple_of(slot * SPAN, SPAN) for slot in slots]
        keys = [kv_ref[pl.ds(start, SPAN), :HEAD_DIM] for start in starts]
        values = [
            jnp.concatenate([kv_ref[pl.ds(start, SPAN), HEAD_DIM:], ones], 1) for start in starts
        ]
        for head in range(heads):
            queries = q_ref[rows, head * HEAD_DIM : (head + 1) * HEAD_DIM]
            scores = [
                lax.dot_general(
                    queries, key, (((1,), (1,)), ((), ())), preferred_element_type=jnp.float32
                )
                for key in keys
            ]
            if first:
                scores[0] = jnp.where(causal, scores[0], NEG_FILL)
            best = functools.reduce(jnp.maximum, scores)
            best = jnp.max(best, axis=1, keepdims=True)
            if first:
                top = jnp.broadcast_to(best, (SPAN, HEAD_DIM))
            else:
                before = top_ref[head]
                top = jnp.maximum(before, best)
            top_ref[head] = top
            wide = jnp.concatenate([top, top], 1)
            added = None
            for score, value in zip(scores, values):
                weight = jnp.exp2((score - wide) * LOG2_SCALE).astype(jnp.bfloat16)
                term = jnp.dot(weight, value, preferred_element_type=jnp.float32)
                added = term if added is None else added + term
            if first:
                total_ref[head] = added
            else:
                factor = jnp.exp2((before - top) * LOG2_SCALE)
                total_ref[head] = total_ref[head] * jnp.concatenate([factor, factor], 1) + added

    def one_run(part, carry):
        rows = pl.ds(pl.multiple_of(part * SPAN, SPAN), SPAN)
        own = own_run(pos_ref, part)
        count = jnp.int32(0)
        for place, mask in enumerate(masks):
            for half in range(2):
                block = pos_ref[(me ^ mask) * (2 * SPAN) + half * SPAN] // SPAN
                order[count] = place * 2 + half
                count = count + (block < own).astype(jnp.int32)
        odd = count % 2

        @pl.when(odd == 0)
        def _():
            visit(rows, [part], True)

        @pl.when(odd == 1)
        def _():
            visit(rows, [part, order[0]], True)

        def pair(step, carry):
            visit(rows, [order[odd + 2 * step], order[odd + 2 * step + 1]], False)
            return carry

        lax.fori_loop(0, count // 2, pair, 0)
        for head in range(heads):
            sums = total_ref[head]
            out_ref[rows, head * HEAD_DIM : (head + 1) * HEAD_DIM] = (
                sums[:, :HEAD_DIM] / sums[:, HEAD_DIM:]
            ).astype(out_ref.dtype)
        return carry

    lax.fori_loop(0, q_ref.shape[0] // SPAN, one_run, 0)


def attend(queries, gathered, positions, masks):
    heads = queries.shape[1] // HEAD_DIM
    vmem = pl.BlockSpec(memory_space=pltpu.VMEM)
    smem = pl.BlockSpec(memory_space=pltpu.SMEM)
    return pl.pallas_call(
        functools.partial(attention_kernel, masks),
        in_specs=[smem, vmem, vmem],
        out_specs=vmem,
        out_shape=jax.ShapeDtypeStruct(queries.shape, jnp.bfloat16),
        scratch_shapes=[
            pltpu.SMEM((2 * len(masks) + 1,), jnp.int32),
            pltpu.VMEM((heads, SPAN, HEAD_DIM), jnp.float32),
            pltpu.VMEM((heads, SPAN, 2 * HEAD_DIM), jnp.float32),
        ],
        compiler_params=pltpu.CompilerParams(vmem_limit_bytes=VMEM_LIMIT),
    )(positions, queries, gathered)


def exchanged(value, mask):
    count = lax.axis_size("outer") * lax.axis_size("inner")
    return lax.ppermute(value, SEQ_AXES, [(source, source ^ mask) for source in range(count)])


def body(tokens, positions, w_query, w_keyval):
    count = lax.axis_size("outer") * lax.axis_size("inner")
    tables = rotation_tables(positions.shape[0] // SPAN)
    stacked = project(tokens, w_keyval, positions, tables, 1, 1024)
    chip_masks = list(range(0, count, 2))
    blocks = [stacked] + [exchanged(stacked, mask) for mask in chip_masks[1:]]
    blocks = blocks + [exchanged(block, 1) for block in blocks]
    masks = chip_masks + [mask ^ 1 for mask in chip_masks]
    queries = project(tokens, w_query, positions, tables, w_query.shape[1] // HEAD_DIM, 1024)
    return attend(queries, jnp.concatenate(blocks, 0), positions, masks)


def solution(mesh):
    placed = (P(SEQ_AXES, None), P(), P(None, "head"), P(None, "head"))
    return jax.shard_map(
        body, mesh=mesh, in_specs=placed, out_specs=P(SEQ_AXES, "head"), check_vma=False
    )
```

```python
import functools
import math

import jax
import jax.numpy as jnp
import numpy as np
from jax import lax
from jax.experimental import pallas as pl
from jax.experimental.pallas import tpu as pltpu
from jax.sharding import PartitionSpec as P

HEAD_DIM = 128
HALF = HEAD_DIM // 2
SPAN = 256
ROPE_BASE = 500000.0
NEG_FILL = -1e30
LOG2_SCALE = math.log2(math.e) / math.sqrt(HEAD_DIM)
MIB = 1024 * 1024
CHUNKS = 8
FIRST_CHUNKS = 4
QUERY_BLOCK = 256
GROUP = 4
SEQ_AXES = ("outer", "inner")


def rotation_tables(runs):
    freqs = ROPE_BASE ** (-(np.arange(HALF, dtype=np.float64) * 2.0) / HEAD_DIM)
    freqs = np.concatenate([freqs, freqs])
    within = np.arange(SPAN, dtype=np.float64)[:, None] * freqs
    starts = (np.arange(runs, dtype=np.float64) * SPAN)[:, None] * freqs
    within = np.stack([np.cos(within), np.sin(within)]).astype(np.float32)
    starts = np.stack([np.cos(starts), np.sin(starts)], 1).astype(np.float32)
    return jnp.asarray(within), jnp.asarray(starts)


def run_rotation(within_ref, starts_ref, run):
    cos_in, sin_in = within_ref[0], within_ref[1]
    start = starts_ref[run]
    cos_at, sin_at = start[0:1], start[1:2]
    lane = lax.broadcasted_iota(jnp.int32, (1, HEAD_DIM), 1)
    sign = jnp.where(lane < HALF, -1.0, 1.0).astype(jnp.float32)
    cosine = cos_in * cos_at - sin_in * sin_at
    sine = (sin_in * cos_at + cos_in * sin_at) * sign
    return cosine, sine


def rotate(rows, cosine, sine):
    return rows * cosine + pltpu.roll(rows, HALF, 1) * sine


def own_run(pos_ref, index):
    row = lax.axis_index("outer") * lax.axis_size("inner") + lax.axis_index("inner")
    return pos_ref[row * (2 * SPAN) + index * SPAN] // SPAN


def keyval_kernel(
    pos_ref, tokens_hbm, w_hbm, within_hbm, starts_hbm, out_ref, tokens_ref, turn_ref, w_ref,
    within_ref, starts_ref, total, table_sems, token_sems, w_sems
):
    rows, width = tokens_ref.shape
    depth = width // CHUNKS
    copies = []
    for chunk in range(CHUNKS):
        part = pl.ds(chunk * depth, depth)
        copies.append(
            (
                pltpu.make_async_copy(
                    tokens_hbm.at[:, part], tokens_ref.at[:, part], token_sems.at[chunk]
                ),
                pltpu.make_async_copy(w_hbm.at[part], w_ref.at[part], w_sems.at[chunk]),
            )
        )
    tables = [
        pltpu.make_async_copy(within_hbm, within_ref, table_sems.at[0]),
        pltpu.make_async_copy(starts_hbm, starts_ref, table_sems.at[1]),
    ]
    for pair in copies:
        for copy in pair:
            copy.start()
    for copy in tables:
        copy.start()
    for chunk, pair in enumerate(copies):
        for copy in pair:
            copy.wait()
        if chunk == 0:
            for copy in tables:
                copy.wait()
            for part in range(rows // SPAN):
                cosine, sine = run_rotation(within_ref, starts_ref, own_run(pos_ref, part))
                turn_ref[0, pl.ds(part * SPAN, SPAN)] = cosine
                turn_ref[1, pl.ds(part * SPAN, SPAN)] = sine
        part = pl.ds(chunk * depth, depth)
        product = jnp.dot(
            tokens_ref[:, part], w_ref[part], preferred_element_type=jnp.float32
        )
        if chunk == 0:
            total[...] = product
        elif chunk < CHUNKS - 1:
            total[...] += product
        else:
            product = total[...] + product
            keys = rotate(product[:, :HEAD_DIM], turn_ref[0], turn_ref[1])
            out_ref[:, :HEAD_DIM] = keys.astype(out_ref.dtype)
            out_ref[:, HEAD_DIM:] = product[:, HEAD_DIM:].astype(out_ref.dtype)


def keyval(tokens, w_keyval, positions, tables):
    rows, width = tokens.shape
    columns = w_keyval.shape[1]
    within, starts = tables
    vmem = pl.BlockSpec(memory_space=pltpu.VMEM)
    anywhere = pl.BlockSpec(memory_space=pltpu.HBM)
    return pl.pallas_call(
        keyval_kernel,
        in_specs=[pl.BlockSpec(memory_space=pltpu.SMEM)] + [anywhere] * 4,
        out_specs=[vmem] * 3,
        out_shape=[
            jax.ShapeDtypeStruct((rows, columns), jnp.bfloat16),
            jax.ShapeDtypeStruct(tokens.shape, tokens.dtype),
            jax.ShapeDtypeStruct((2, rows, HEAD_DIM), jnp.float32),
        ],
        scratch_shapes=[
            pltpu.VMEM(w_keyval.shape, w_keyval.dtype),
            pltpu.VMEM(within.shape, within.dtype),
            pltpu.VMEM(starts.shape, starts.dtype),
            pltpu.VMEM((rows, columns), jnp.float32),
            pltpu.SemaphoreType.DMA((2,)),
            pltpu.SemaphoreType.DMA((CHUNKS,)),
            pltpu.SemaphoreType.DMA((CHUNKS,)),
        ],
        compiler_params=pltpu.CompilerParams(vmem_limit_bytes=16 * MIB),
        cost_estimate=pl.CostEstimate(
            flops=2 * rows * width * columns,
            bytes_accessed=2 * (rows * width + width * columns),
            transcendentals=0,
        ),
    )(positions, tokens, w_keyval, within, starts)


def query_kernel(tokens_ref, turn_ref, w_hbm, out_ref, w_ref, sems):
    rows, width = tokens_ref.shape
    blocks = out_ref.shape[1] // QUERY_BLOCK
    depth = width // FIRST_CHUNKS

    def block_copy(block):
        cols = pl.ds(block * QUERY_BLOCK, QUERY_BLOCK)
        return pltpu.make_async_copy(
            w_hbm.at[:, cols], w_ref.at[block], sems.at[FIRST_CHUNKS + block]
        )

    first = [
        pltpu.make_async_copy(
            w_hbm.at[pl.ds(chunk * depth, depth), pl.ds(0, QUERY_BLOCK)],
            w_ref.at[0, pl.ds(chunk * depth, depth)],
            sems.at[chunk],
        )
        for chunk in range(FIRST_CHUNKS)
    ]
    for copy in first:
        copy.start()
    for block in range(1, blocks):
        block_copy(block).start()

    def finish(start, product):
        for head in range(QUERY_BLOCK // HEAD_DIM):
            piece = rotate(
                product[:, head * HEAD_DIM : (head + 1) * HEAD_DIM], turn_ref[0], turn_ref[1]
            )
            out_ref[:, pl.ds(start + head * HEAD_DIM, HEAD_DIM)] = piece.astype(out_ref.dtype)

    product = None
    for chunk, copy in enumerate(first):
        copy.wait()
        part = pl.ds(chunk * depth, depth)
        term = jnp.dot(tokens_ref[:, part], w_ref[0, part], preferred_element_type=jnp.float32)
        product = term if product is None else product + term
    finish(0, product)

    def one_block(block, carry):
        block_copy(block).wait()
        product = jnp.dot(tokens_ref[...], w_ref[block], preferred_element_type=jnp.float32)
        finish(pl.multiple_of(block * QUERY_BLOCK, QUERY_BLOCK), product)
        return carry

    lax.fori_loop(1, blocks, one_block, 0)


def project_queries(tokens, turn, w_query):
    rows, width = tokens.shape
    columns = w_query.shape[1]
    blocks = columns // QUERY_BLOCK
    vmem = pl.BlockSpec(memory_space=pltpu.VMEM)
    return pl.pallas_call(
        query_kernel,
        in_specs=[vmem, vmem, pl.BlockSpec(memory_space=pltpu.HBM)],
        out_specs=vmem,
        out_shape=jax.ShapeDtypeStruct((rows, columns), jnp.bfloat16),
        scratch_shapes=[
            pltpu.VMEM((blocks, width, QUERY_BLOCK), w_query.dtype),
            pltpu.SemaphoreType.DMA((FIRST_CHUNKS + blocks,)),
        ],
        compiler_params=pltpu.CompilerParams(vmem_limit_bytes=28 * MIB),
        cost_estimate=pl.CostEstimate(
            flops=2 * rows * width * columns,
            bytes_accessed=2 * width * columns,
            transcendentals=0,
        ),
    )(tokens, turn, w_query)


def attention_kernel(masks, pos_ref, q_ref, kv_ref, out_ref, order, top_ref, total_ref):
    heads = q_ref.shape[1] // HEAD_DIM
    me = lax.axis_index("outer") * lax.axis_size("inner") + lax.axis_index("inner")
    causal = lax.broadcasted_iota(jnp.int32, (SPAN, SPAN), 1) <= lax.broadcasted_iota(
        jnp.int32, (SPAN, SPAN), 0
    )
    ones = jnp.ones((SPAN, HEAD_DIM), jnp.bfloat16)

    def visit(rows, slots, first):
        starts = [pl.multiple_of(slot * SPAN, SPAN) for slot in slots]
        keys = [kv_ref[pl.ds(start, SPAN), :HEAD_DIM] for start in starts]
        values = [
            jnp.concatenate([kv_ref[pl.ds(start, SPAN), HEAD_DIM:], ones], 1) for start in starts
        ]
        def dots(head):
            queries = q_ref[rows, head * HEAD_DIM : (head + 1) * HEAD_DIM]
            return [
                lax.dot_general(
                    queries, key, (((1,), (1,)), ((), ())), preferred_element_type=jnp.float32
                )
                for key in keys
            ]

        def soften(head, scores):
            if first:
                scores[0] = jnp.where(causal, scores[0], NEG_FILL)
            best = functools.reduce(jnp.maximum, scores)
            best = jnp.max(best, axis=1, keepdims=True)
            if first:
                top = jnp.broadcast_to(best, (SPAN, HEAD_DIM))
                factor = None
            else:
                before = top_ref[head]
                top = jnp.maximum(before, best)
                factor = jnp.exp2((before - top) * LOG2_SCALE)
            top_ref[head] = top
            wide = jnp.concatenate([top, top], 1)
            return [jnp.exp2((score - wide) * LOG2_SCALE).astype(jnp.bfloat16) for score in scores], factor

        def add(head, weights, factor):
            added = jnp.dot(jnp.concatenate(weights, 1), jnp.concatenate(values, 0), preferred_element_type=jnp.float32)
            if first:
                total_ref[head] = added
            else:
                total_ref[head] = total_ref[head] * jnp.concatenate([factor, factor], 1) + added

        ahead = 2
        waiting = [dots(h) for h in range(min(ahead, heads))]
        soft = []
        for head in range(heads):
            if head + ahead < heads: waiting.append(dots(head + ahead))
            soft.append(soften(head, waiting[head]))
            if head >= 1: add(head - 1, *soft[head - 1])
        add(heads - 1, *soft[heads - 1])

    def one_run(part, carry):
        rows = pl.ds(pl.multiple_of(part * SPAN, SPAN), SPAN)
        own = own_run(pos_ref, part)
        count = jnp.int32(0)
        for place, mask in enumerate(masks):
            for half in range(2):
                block = pos_ref[(me ^ mask) * (2 * SPAN) + half * SPAN] // SPAN
                order[count] = place * 2 + half
                count = count + (block < own).astype(jnp.int32)
        odd = count % GROUP
        for extra in range(GROUP):
            @pl.when(odd == extra)
            def _():
                visit(rows, [part] + [order[i] for i in range(extra)], True)

        def several(step, carry):
            visit(rows, [order[odd + GROUP * step + i] for i in range(GROUP)], False)
            return carry

        lax.fori_loop(0, count // GROUP, several, 0)
        for head in range(heads):
            sums = total_ref[head]
            out_ref[rows, head * HEAD_DIM : (head + 1) * HEAD_DIM] = (
                sums[:, :HEAD_DIM] / sums[:, HEAD_DIM:]
            ).astype(out_ref.dtype)
        return carry

    lax.fori_loop(0, q_ref.shape[0] // SPAN, one_run, 0)


def attend(queries, gathered, positions, masks):
    heads = queries.shape[1] // HEAD_DIM
    vmem = pl.BlockSpec(memory_space=pltpu.VMEM)
    smem = pl.BlockSpec(memory_space=pltpu.SMEM)
    return pl.pallas_call(
        functools.partial(attention_kernel, masks),
        in_specs=[smem, vmem, vmem],
        out_specs=vmem,
        out_shape=jax.ShapeDtypeStruct(queries.shape, jnp.bfloat16),
        scratch_shapes=[
            pltpu.SMEM((2 * len(masks) + 1,), jnp.int32),
            pltpu.VMEM((heads, SPAN, HEAD_DIM), jnp.float32),
            pltpu.VMEM((heads, SPAN, 2 * HEAD_DIM), jnp.float32),
        ],
        compiler_params=pltpu.CompilerParams(vmem_limit_bytes=32 * MIB),
    )(positions, queries, gathered)


def exchanged(value, mask):
    count = lax.axis_size("outer") * lax.axis_size("inner")
    return lax.ppermute(value, SEQ_AXES, [(source, source ^ mask) for source in range(count)])


def body(tokens, positions, w_query, w_keyval):
    count = lax.axis_size("outer") * lax.axis_size("inner")
    tables = rotation_tables(positions.shape[0] // SPAN)
    stacked, kept, turn = keyval(tokens, w_keyval, positions, tables)
    chip_masks = list(range(0, count, 2))
    blocks = [stacked] + [exchanged(stacked, mask) for mask in chip_masks[1:]]
    blocks = blocks + [exchanged(block, 1) for block in blocks]
    masks = chip_masks + [mask ^ 1 for mask in chip_masks]
    queries = project_queries(kept, turn, w_query)
    return attend(queries, jnp.concatenate(blocks, 0), positions, masks)


def solution(mesh):
    placed = (P(SEQ_AXES, None), P(), P(None, "head"), P(None, "head"))
    return jax.shard_map(
        body, mesh=mesh, in_specs=placed, out_specs=P(SEQ_AXES, "head"), check_vma=False
    )
```

```python
import functools
import math

import jax
import jax.numpy as jnp
import numpy as np
from jax import lax
from jax.experimental import pallas as pl
from jax.experimental.pallas import tpu as pltpu
from jax.sharding import PartitionSpec as P

HEAD_DIM = 128
HALF = HEAD_DIM // 2
SPAN = 256
ROPE_BASE = 500000.0
NEG_FILL = -1e30
LOG2_SCALE = math.log2(math.e) / math.sqrt(HEAD_DIM)
MIB = 1024 * 1024
VMEM_LIMIT = 58 * MIB
BLOCK = 256
DEPTH = 1024
WINDOW = 3
GROUP = 4
AHEAD = 2
SEQ_AXES = ("outer", "inner")


def rotation_tables(runs):
    freqs = ROPE_BASE ** (-(np.arange(HALF, dtype=np.float64) * 2.0) / HEAD_DIM)
    freqs = np.concatenate([freqs, freqs])
    within = np.arange(SPAN, dtype=np.float64)[:, None] * freqs
    starts = (np.arange(runs, dtype=np.float64) * SPAN)[:, None] * freqs
    within = np.stack([np.cos(within), np.sin(within)]).astype(np.float32)
    starts = np.stack([np.cos(starts), np.sin(starts)], 1).astype(np.float32)
    return jnp.asarray(within), jnp.asarray(starts)


def run_rotation(within_ref, starts_ref, run):
    cos_in, sin_in = within_ref[0], within_ref[1]
    start = starts_ref[run]
    cos_at, sin_at = start[0:1], start[1:2]
    lane = lax.broadcasted_iota(jnp.int32, (1, HEAD_DIM), 1)
    sign = jnp.where(lane < HALF, -1.0, 1.0).astype(jnp.float32)
    cosine = cos_in * cos_at - sin_in * sin_at
    sine = (sin_in * cos_at + cos_in * sin_at) * sign
    return cosine, sine


def rotate(rows, cosine, sine):
    return rows * cosine + pltpu.roll(rows, HALF, 1) * sine


def own_run(pos_ref, index):
    row = lax.axis_index("outer") * lax.axis_size("inner") + lax.axis_index("inner")
    return pos_ref[row * (2 * SPAN) + index * SPAN] // SPAN


def projection_kernel(
    depths, rotated, pos_ref, tokens_hbm, w_hbm, within_hbm, starts_hbm, out_ref, tokens_ref,
    w_ref, within_ref, starts_ref, total, turn_ref, table_sems, token_sems, w_sems
):
    rows, columns = out_ref.shape
    parts, start = [], 0
    for depth in depths:
        parts.append(pl.ds(start, depth))
        start += depth
    copies = [
        (
            pltpu.make_async_copy(
                tokens_hbm.at[:, part], tokens_ref.at[:, part], token_sems.at[chunk]
            ),
            pltpu.make_async_copy(w_hbm.at[part], w_ref.at[part], w_sems.at[chunk]),
        )
        for chunk, part in enumerate(parts)
    ]
    tables = [
        pltpu.make_async_copy(within_hbm, within_ref, table_sems.at[0]),
        pltpu.make_async_copy(starts_hbm, starts_ref, table_sems.at[1]),
    ]
    for pair in copies[:WINDOW]:
        for copy in pair:
            copy.start()
    for copy in tables:
        copy.start()

    for chunk, (part, pair) in enumerate(zip(parts, copies)):
        for copy in pair:
            copy.wait()
        if chunk + WINDOW < len(parts):
            for copy in copies[chunk + WINDOW]:
                copy.start()
        if chunk == 1:
            for copy in tables:
                copy.wait()
            for run in range(rows // SPAN):
                cosine, sine = run_rotation(within_ref, starts_ref, own_run(pos_ref, run))
                turn_ref[0, pl.ds(run * SPAN, SPAN)] = cosine
                turn_ref[1, pl.ds(run * SPAN, SPAN)] = sine
        if chunk < len(parts) - 1:
            product = jnp.dot(
                tokens_ref[:, part], w_ref[part], preferred_element_type=jnp.float32
            )
            total[...] = product if chunk == 0 else total[...] + product
            continue
        for block in range(columns // BLOCK):
            cols = pl.ds(block * BLOCK, BLOCK)
            product = total[:, cols] + jnp.dot(
                tokens_ref[:, part], w_ref[part, cols], preferred_element_type=jnp.float32
            )
            for head in range(BLOCK // HEAD_DIM):
                piece = product[:, head * HEAD_DIM : (head + 1) * HEAD_DIM]
                place = block * BLOCK + head * HEAD_DIM
                if place < rotated:
                    piece = rotate(piece, turn_ref[0], turn_ref[1])
                out_ref[:, place : place + HEAD_DIM] = piece.astype(out_ref.dtype)


def project(tokens, weights, positions, tables, rotated):
    rows, width = tokens.shape
    depths = (DEPTH,) * (width // DEPTH)
    columns = weights.shape[1]
    within, starts = tables
    return pl.pallas_call(
        functools.partial(projection_kernel, depths, rotated),
        in_specs=[pl.BlockSpec(memory_space=pltpu.SMEM)]
        + [pl.BlockSpec(memory_space=pltpu.HBM)] * 4,
        out_specs=pl.BlockSpec(memory_space=pltpu.VMEM),
        out_shape=jax.ShapeDtypeStruct((rows, columns), jnp.bfloat16),
        scratch_shapes=[
            pltpu.VMEM(tokens.shape, tokens.dtype),
            pltpu.VMEM(weights.shape, weights.dtype),
            pltpu.VMEM(within.shape, within.dtype),
            pltpu.VMEM(starts.shape, starts.dtype),
            pltpu.VMEM((rows, columns), jnp.float32),
            pltpu.VMEM((2, rows, HEAD_DIM), jnp.float32),
            pltpu.SemaphoreType.DMA((2,)),
            pltpu.SemaphoreType.DMA((len(depths),)),
            pltpu.SemaphoreType.DMA((len(depths),)),
        ],
        compiler_params=pltpu.CompilerParams(vmem_limit_bytes=VMEM_LIMIT),
        cost_estimate=pl.CostEstimate(
            flops=2 * rows * width * columns,
            bytes_accessed=2 * (rows * width + width * columns),
            transcendentals=0,
        ),
    )(positions, tokens, weights, within, starts)


def attention_kernel(masks, last, pos_ref, q_ref, kv_ref, *refs):
    if last:
        _, _, out_ref, top_ref, total_ref, order = refs
    else:
        top_ref, total_ref, order = refs
    heads = q_ref.shape[1] // HEAD_DIM
    me = lax.axis_index("outer") * lax.axis_size("inner") + lax.axis_index("inner")
    causal = lax.broadcasted_iota(jnp.int32, (SPAN, SPAN), 1) <= lax.broadcasted_iota(
        jnp.int32, (SPAN, SPAN), 0
    )
    ones = jnp.ones((SPAN, HEAD_DIM), jnp.bfloat16)

    def visit(part, slots, first):
        rows = pl.ds(pl.multiple_of(part * SPAN, SPAN), SPAN)
        starts = [pl.multiple_of(slot * SPAN, SPAN) for slot in slots]
        keys = [kv_ref[pl.ds(start, SPAN), :HEAD_DIM] for start in starts]
        values = jnp.concatenate(
            [
                jnp.concatenate([kv_ref[pl.ds(start, SPAN), HEAD_DIM:], ones], 1)
                for start in starts
            ],
            0,
        )

        def score(head):
            queries = q_ref[rows, head * HEAD_DIM : (head + 1) * HEAD_DIM]
            return [
                lax.dot_general(
                    queries, key, (((1,), (1,)), ((), ())), preferred_element_type=jnp.float32
                )
                for key in keys
            ]

        def weigh(head, scores):
            if first:
                scores[0] = jnp.where(causal, scores[0], NEG_FILL)
            best = jnp.max(functools.reduce(jnp.maximum, scores), axis=1, keepdims=True)
            if first:
                top, factor = jnp.broadcast_to(best, (SPAN, HEAD_DIM)), None
            else:
                before = top_ref[part, head]
                top = jnp.maximum(before, best)
                factor = jnp.exp2((before - top) * LOG2_SCALE)
            top_ref[part, head] = top
            wide = jnp.concatenate([top, top], 1)
            weights = [
                jnp.exp2((piece - wide) * LOG2_SCALE).astype(jnp.bfloat16) for piece in scores
            ]
            return jnp.concatenate(weights, 1), factor

        def add(head, weights, factor):
            added = jnp.dot(weights, values, preferred_element_type=jnp.float32)
            if first:
                total_ref[part, head] = added
            else:
                total_ref[part, head] = (
                    total_ref[part, head] * jnp.concatenate([factor, factor], 1) + added
                )

        scores = [score(head) for head in range(AHEAD)]
        weighed = None
        for head in range(heads):
            if head + AHEAD < heads:
                scores.append(score(head + AHEAD))
            following = weigh(head, scores[head])
            if head:
                add(head - 1, *weighed)
            weighed = following
        add(heads - 1, *weighed)

    def one_run(part, carry):
        own = own_run(pos_ref, part)
        count = jnp.int32(0)
        for place, mask in enumerate(masks):
            for half in range(2):
                block = pos_ref[(me ^ mask) * (2 * SPAN) + half * SPAN] // SPAN
                order[count] = place * 2 + half
                count = count + (block < own).astype(jnp.int32)
        odd = count % GROUP
        for extra in range(last, GROUP):

            @pl.when(odd == extra)
            def _():
                slots = [order[place] for place in range(extra)]
                visit(part, slots if last else [part] + slots, not last)

        def several(step, carry):
            visit(part, [order[odd + GROUP * step + place] for place in range(GROUP)], False)
            return carry

        lax.fori_loop(0, count // GROUP, several, 0)
        if last:
            rows = pl.ds(pl.multiple_of(part * SPAN, SPAN), SPAN)
            for head in range(heads):
                sums = total_ref[part, head]
                out_ref[rows, head * HEAD_DIM : (head + 1) * HEAD_DIM] = (
                    sums[:, :HEAD_DIM] / sums[:, HEAD_DIM:]
                ).astype(out_ref.dtype)
        return carry

    lax.fori_loop(0, q_ref.shape[0] // SPAN, one_run, 0)


def attend(queries, pieces, positions, masks, state=()):
    last = bool(state)
    heads = queries.shape[1] // HEAD_DIM
    runs = queries.shape[0] // SPAN
    vmem = pl.BlockSpec(memory_space=pltpu.VMEM)
    smem = pl.BlockSpec(memory_space=pltpu.SMEM)
    shapes = [
        jax.ShapeDtypeStruct((runs, heads, SPAN, HEAD_DIM), jnp.float32),
        jax.ShapeDtypeStruct((runs, heads, SPAN, 2 * HEAD_DIM), jnp.float32),
    ]
    aliases = {}
    if last:
        shapes = [jax.ShapeDtypeStruct(queries.shape, jnp.bfloat16)] + shapes
        aliases = {3: 1, 4: 2}
    return pl.pallas_call(
        functools.partial(attention_kernel, masks, last),
        in_specs=[smem, vmem, vmem] + [vmem] * len(state),
        out_specs=[vmem] * len(shapes),
        out_shape=shapes,
        input_output_aliases=aliases,
        scratch_shapes=[pltpu.SMEM((2 * len(masks) + 1,), jnp.int32)],
        compiler_params=pltpu.CompilerParams(vmem_limit_bytes=24 * MIB),
    )(positions, queries, pieces, *state)


def exchanged(value, mask):
    count = lax.axis_size("outer") * lax.axis_size("inner")
    return lax.ppermute(value, SEQ_AXES, [(source, source ^ mask) for source in range(count)])


def body(tokens, positions, w_query, w_keyval):
    count = lax.axis_size("outer") * lax.axis_size("inner")
    tables = rotation_tables(positions.shape[0] // SPAN)
    masks = list(range(0, count, 2))
    stacked = project(tokens, w_keyval, positions, tables, HEAD_DIM)
    direct = [stacked] + [exchanged(stacked, mask) for mask in masks[1:]]
    queries = project(tokens, w_query, positions, tables, w_query.shape[1])
    queries, *direct = lax.optimization_barrier([queries, *direct])
    direct = jnp.concatenate(direct, 0)
    relayed = exchanged(direct, 1)
    state = attend(queries, direct, positions, masks)
    return attend(queries, relayed, positions, [mask ^ 1 for mask in masks], state)[0]


def solution(mesh):
    placed = (P(SEQ_AXES, None), P(), P(None, "head"), P(None, "head"))
    return jax.shard_map(
        body, mesh=mesh, in_specs=placed, out_specs=P(SEQ_AXES, "head"), check_vma=False
    )
```

```python
import functools
import math

import jax
import jax.numpy as jnp
import numpy as np
from jax import lax
from jax.experimental import pallas as pl
from jax.experimental.pallas import tpu as pltpu
from jax.sharding import PartitionSpec as P

HEAD_DIM = 128
HALF = HEAD_DIM // 2
SPAN = 256
ROPE_BASE = 500000.0
NEG_FILL = -1e30
LOG2_SCALE = math.log2(math.e) / math.sqrt(HEAD_DIM)
MIB = 1024 * 1024
BLOCK = 256
DEPTH = 1024
WINDOW = 3
GROUP = 4
AHEAD = 2
SEQ_AXES = ("outer", "inner")


def rotation_tables(runs):
    freqs = ROPE_BASE ** (-(np.arange(HALF, dtype=np.float64) * 2.0) / HEAD_DIM)
    freqs = np.concatenate([freqs, freqs])
    within = np.arange(SPAN, dtype=np.float64)[:, None] * freqs
    starts = (np.arange(runs, dtype=np.float64) * SPAN)[:, None] * freqs
    within = np.stack([np.cos(within), np.sin(within)]).astype(np.float32)
    starts = np.stack([np.cos(starts), np.sin(starts)], 1).astype(np.float32)
    return jnp.asarray(within), jnp.asarray(starts)


def run_rotation(within_ref, starts_ref, run):
    cos_in, sin_in = within_ref[0], within_ref[1]
    start = starts_ref[run]
    cos_at, sin_at = start[0:1], start[1:2]
    lane = lax.broadcasted_iota(jnp.int32, (SPAN, HEAD_DIM), 1)
    cosine = cos_in * cos_at - sin_in * sin_at
    sine = sin_in * cos_at + cos_in * sin_at
    return jnp.where(lane < HALF, cosine, sine)


def spread(turn):
    lane = lax.broadcasted_iota(jnp.int32, turn.shape, 1)
    other = pltpu.roll(turn, HALF, 1)
    return jnp.where(lane < HALF, turn, other), jnp.where(lane < HALF, -other, turn)


def rotate(rows, cosine, sine):
    return rows * cosine + pltpu.roll(rows, HALF, 1) * sine


def own_run(pos_ref, index):
    row = lax.axis_index("outer") * lax.axis_size("inner") + lax.axis_index("inner")
    return pos_ref[row * (2 * SPAN) + index * SPAN] // SPAN


def accumulate(tokens_hbm, w_hbm, tokens_ref, w_ref, total, token_sems, w_sems, beside, finish):
    width, columns = w_ref.shape
    chunks = width // DEPTH
    parts = [pl.ds(chunk * DEPTH, DEPTH) for chunk in range(chunks)]
    copies = [
        (
            pltpu.make_async_copy(
                tokens_hbm.at[:, part], tokens_ref.at[:, part], token_sems.at[chunk]
            ),
            pltpu.make_async_copy(w_hbm.at[part], w_ref.at[part], w_sems.at[chunk]),
        )
        for chunk, part in enumerate(parts)
    ]
    for pair in copies[:WINDOW]:
        for copy in pair:
            copy.start()
    for chunk, (part, pair) in enumerate(zip(parts, copies)):
        for copy in pair:
            copy.wait()
        if chunk + WINDOW < chunks:
            for copy in copies[chunk + WINDOW]:
                copy.start()
        if chunk == 1:
            beside()
        if chunk < chunks - 1:
            product = jnp.dot(
                tokens_ref[:, part], w_ref[part], preferred_element_type=jnp.float32
            )
            total[...] = product if chunk == 0 else total[...] + product
            continue
        for block in range(columns // BLOCK):
            cols = pl.ds(block * BLOCK, BLOCK)
            product = total[:, cols] + jnp.dot(
                tokens_ref[:, part], w_ref[part, cols], preferred_element_type=jnp.float32
            )
            for head in range(BLOCK // HEAD_DIM):
                finish(
                    block * BLOCK + head * HEAD_DIM,
                    product[:, head * HEAD_DIM : (head + 1) * HEAD_DIM],
                )


def keyval_kernel(
    pos_hbm, within_hbm, starts_hbm, tokens_hbm, w_hbm, out_ref, turn_ref, tokens_ref, w_ref, total,
    token_sems, w_sems, pos_ref, within_ref, starts_ref, table_sems
):
    tables = [
        pltpu.make_async_copy(pos_hbm, pos_ref, table_sems.at[0]),
        pltpu.make_async_copy(within_hbm, within_ref, table_sems.at[1]),
        pltpu.make_async_copy(starts_hbm, starts_ref, table_sems.at[2]),
    ]
    for copy in tables:
        copy.start()

    def beside():
        for copy in tables:
            copy.wait()
        for run in range(out_ref.shape[0] // SPAN):
            turn_ref[pl.ds(run * SPAN, SPAN)] = run_rotation(
                within_ref, starts_ref, own_run(pos_ref, run)
            )

    def finish(place, piece):
        if place < HEAD_DIM:
            piece = rotate(piece, *spread(turn_ref[...]))
        out_ref[:, place : place + HEAD_DIM] = piece.astype(out_ref.dtype)

    accumulate(
        tokens_hbm, w_hbm, tokens_ref, w_ref, total, token_sems, w_sems, beside, finish
    )


def query_kernel(
    turn_ref, tokens_hbm, w_hbm, out_ref, tokens_ref, w_ref, total, token_sems, w_sems
):
    def finish(place, piece):
        piece = rotate(piece, *spread(turn_ref[...]))
        out_ref[:, place : place + HEAD_DIM] = piece.astype(out_ref.dtype)

    accumulate(
        tokens_hbm, w_hbm, tokens_ref, w_ref, total, token_sems, w_sems, lambda: None, finish
    )


def project(kernel, others, tokens, weights, more_out, more_scratch, limit):
    rows, width = tokens.shape
    columns = weights.shape[1]
    vmem = pl.BlockSpec(memory_space=pltpu.VMEM)
    hbm = pl.BlockSpec(memory_space=pltpu.HBM)
    return pl.pallas_call(
        kernel,
        in_specs=[vmem if len(others) == 1 else hbm] * len(others) + [hbm] * 2,
        out_specs=[vmem] * (1 + len(more_out)),
        out_shape=[jax.ShapeDtypeStruct((rows, columns), jnp.bfloat16)] + more_out,
        scratch_shapes=[
            pltpu.VMEM(tokens.shape, tokens.dtype),
            pltpu.VMEM(weights.shape, weights.dtype),
            pltpu.VMEM((rows, columns), jnp.float32),
            pltpu.SemaphoreType.DMA((width // DEPTH,)),
            pltpu.SemaphoreType.DMA((width // DEPTH,)),
        ]
        + more_scratch,
        compiler_params=pltpu.CompilerParams(vmem_limit_bytes=limit * MIB),
        cost_estimate=pl.CostEstimate(
            flops=2 * rows * width * columns,
            bytes_accessed=2 * (rows * width + width * columns),
            transcendentals=0,
        ),
    )(*others, tokens, weights)


def keyval(tokens, w_keyval, positions):
    within, starts = rotation_tables(positions.shape[0] // SPAN)
    return project(
        keyval_kernel,
        [positions, within, starts],
        tokens,
        w_keyval,
        [jax.ShapeDtypeStruct((tokens.shape[0], HEAD_DIM), jnp.float32)],
        [
            pltpu.SMEM(positions.shape, positions.dtype),
            pltpu.VMEM(within.shape, within.dtype),
            pltpu.VMEM(starts.shape, starts.dtype),
            pltpu.SemaphoreType.DMA((3,)),
        ],
        58,
    )


def attention_kernel(masks, last, pos_ref, q_ref, kv_ref, *refs):
    if last:
        _, _, out_ref, top_ref, total_ref, order = refs
    else:
        top_ref, total_ref, order = refs
    heads = q_ref.shape[1] // HEAD_DIM
    me = lax.axis_index("outer") * lax.axis_size("inner") + lax.axis_index("inner")
    causal = lax.broadcasted_iota(jnp.int32, (SPAN, SPAN), 1) <= lax.broadcasted_iota(
        jnp.int32, (SPAN, SPAN), 0
    )
    ones = jnp.ones((SPAN, HEAD_DIM), jnp.bfloat16)

    def visit(part, slots, first):
        rows = pl.ds(pl.multiple_of(part * SPAN, SPAN), SPAN)
        starts = [pl.multiple_of(slot * SPAN, SPAN) for slot in slots]
        keys = [kv_ref[pl.ds(start, SPAN), :HEAD_DIM] for start in starts]
        values = jnp.concatenate(
            [
                jnp.concatenate([kv_ref[pl.ds(start, SPAN), HEAD_DIM:], ones], 1)
                for start in starts
            ],
            0,
        )

        def score(head):
            queries = q_ref[rows, head * HEAD_DIM : (head + 1) * HEAD_DIM]
            return [
                lax.dot_general(
                    queries, key, (((1,), (1,)), ((), ())), preferred_element_type=jnp.float32
                )
                for key in keys
            ]

        def weigh(head, scores):
            if first:
                scores[0] = jnp.where(causal, scores[0], NEG_FILL)
            best = jnp.max(functools.reduce(jnp.maximum, scores), axis=1, keepdims=True)
            if first:
                top, factor = jnp.broadcast_to(best, (SPAN, HEAD_DIM)), None
            else:
                before = top_ref[part, head]
                top = jnp.maximum(before, best)
                factor = jnp.exp2((before - top) * LOG2_SCALE)
            top_ref[part, head] = top
            wide = jnp.concatenate([top, top], 1)
            weights = [
                jnp.exp2((piece - wide) * LOG2_SCALE).astype(jnp.bfloat16) for piece in scores
            ]
            return jnp.concatenate(weights, 1), factor

        def add(head, weights, factor):
            added = jnp.dot(weights, values, preferred_element_type=jnp.float32)
            if first:
                total_ref[part, head] = added
            else:
                total_ref[part, head] = (
                    total_ref[part, head] * jnp.concatenate([factor, factor], 1) + added
                )

        scores = [score(head) for head in range(AHEAD)]
        weighed = None
        for head in range(heads):
            if head + AHEAD < heads:
                scores.append(score(head + AHEAD))
            following = weigh(head, scores[head])
            if head:
                add(head - 1, *weighed)
            weighed = following
        add(heads - 1, *weighed)

    def one_run(part, carry):
        own = own_run(pos_ref, part)
        count = jnp.int32(0)
        for place, mask in enumerate(masks):
            for half in range(2):
                block = pos_ref[(me ^ mask) * (2 * SPAN) + half * SPAN] // SPAN
                order[count] = place * 2 + half
                count = count + (block < own).astype(jnp.int32)
        odd = count % GROUP
        for extra in range(last, GROUP):

            @pl.when(odd == extra)
            def _():
                slots = [order[place] for place in range(extra)]
                visit(part, slots if last else [part] + slots, not last)

        def several(step, carry):
            visit(part, [order[odd + GROUP * step + place] for place in range(GROUP)], False)
            return carry

        lax.fori_loop(0, count // GROUP, several, 0)
        if last:
            rows = pl.ds(pl.multiple_of(part * SPAN, SPAN), SPAN)
            for head in range(heads):
                sums = total_ref[part, head]
                out_ref[rows, head * HEAD_DIM : (head + 1) * HEAD_DIM] = (
                    sums[:, :HEAD_DIM] / sums[:, HEAD_DIM:]
                ).astype(out_ref.dtype)
        return carry

    lax.fori_loop(0, q_ref.shape[0] // SPAN, one_run, 0)


def attend(queries, pieces, positions, masks, state=()):
    last = bool(state)
    heads = queries.shape[1] // HEAD_DIM
    runs = queries.shape[0] // SPAN
    vmem = pl.BlockSpec(memory_space=pltpu.VMEM)
    smem = pl.BlockSpec(memory_space=pltpu.SMEM)
    shapes = [
        jax.ShapeDtypeStruct((runs, heads, SPAN, HEAD_DIM), jnp.float32),
        jax.ShapeDtypeStruct((runs, heads, SPAN, 2 * HEAD_DIM), jnp.float32),
    ]
    aliases = {}
    if last:
        shapes = [jax.ShapeDtypeStruct(queries.shape, jnp.bfloat16)] + shapes
        aliases = {3: 1, 4: 2}
    return pl.pallas_call(
        functools.partial(attention_kernel, masks, last),
        in_specs=[smem, vmem, vmem] + [vmem] * len(state),
        out_specs=[vmem] * len(shapes),
        out_shape=shapes,
        input_output_aliases=aliases,
        scratch_shapes=[pltpu.SMEM((2 * len(masks) + 1,), jnp.int32)],
        compiler_params=pltpu.CompilerParams(vmem_limit_bytes=24 * MIB),
    )(positions, queries, pieces, *state)


def exchanged(value, mask):
    count = lax.axis_size("outer") * lax.axis_size("inner")
    return lax.ppermute(value, SEQ_AXES, [(source, source ^ mask) for source in range(count)])


def body(tokens, positions, w_query, w_keyval):
    count = lax.axis_size("outer") * lax.axis_size("inner")
    masks = list(range(0, count, 2))
    stacked, turn = keyval(tokens, w_keyval, positions)
    direct = [stacked] + [exchanged(stacked, mask) for mask in masks[1:]]
    queries = project(query_kernel, [turn], tokens, w_query, [], [], 52)[0]
    queries, *direct = lax.optimization_barrier([queries, *direct])
    direct = jnp.concatenate(direct, 0)
    relayed = exchanged(direct, 1)
    state = attend(queries, direct, positions, masks)
    return attend(queries, relayed, positions, [mask ^ 1 for mask in masks], state)[0]


def solution(mesh):
    placed = (P(SEQ_AXES, None), P(), P(None, "head"), P(None, "head"))
    return jax.shard_map(
        body, mesh=mesh, in_specs=placed, out_specs=P(SEQ_AXES, "head"), check_vma=False
    )
```

```python
import functools
import math

import jax
import jax.numpy as jnp
import numpy as np
from jax import lax
from jax.experimental import pallas as pl
from jax.experimental.pallas import tpu as pltpu
from jax.sharding import PartitionSpec as P

HEAD_DIM = 128
HALF = HEAD_DIM // 2
SPAN = 256
ROPE_BASE = 500000.0
NEG_FILL = -1e30
LOG2_SCALE = math.log2(math.e) / math.sqrt(HEAD_DIM)
MIB = 1024 * 1024
BLOCK = 256
DEPTH = 1024
WINDOW = 3
GROUP = 4
AHEAD = 1
PACK = 4
SEQ_AXES = ("outer", "inner")


def rotation_tables(runs):
    freqs = ROPE_BASE ** (-(np.arange(HALF, dtype=np.float64) * 2.0) / HEAD_DIM)
    freqs = np.concatenate([freqs, freqs])
    within = np.arange(SPAN, dtype=np.float64)[:, None] * freqs
    starts = (np.arange(runs, dtype=np.float64) * SPAN)[:, None] * freqs
    within = np.stack([np.cos(within), np.sin(within)]).astype(np.float32)
    starts = np.stack([np.cos(starts), np.sin(starts)], 1).astype(np.float32)
    return jnp.asarray(within), jnp.asarray(starts)


def run_rotation(within_ref, starts_ref, run):
    cos_in, sin_in = within_ref[0], within_ref[1]
    start = starts_ref[run]
    cos_at, sin_at = start[0:1], start[1:2]
    lane = lax.broadcasted_iota(jnp.int32, (SPAN, HEAD_DIM), 1)
    cosine = cos_in * cos_at - sin_in * sin_at
    sine = sin_in * cos_at + cos_in * sin_at
    return jnp.where(lane < HALF, cosine, sine)


def spread(turn):
    lane = lax.broadcasted_iota(jnp.int32, turn.shape, 1)
    other = pltpu.roll(turn, HALF, 1)
    return jnp.where(lane < HALF, turn, other), jnp.where(lane < HALF, -other, turn)


def rotate(rows, cosine, sine):
    return rows * cosine + pltpu.roll(rows, HALF, 1) * sine


def own_run(pos_ref, index):
    row = lax.axis_index("outer") * lax.axis_size("inner") + lax.axis_index("inner")
    return pos_ref[row * (2 * SPAN) + index * SPAN] // SPAN


def accumulate(
    depths, tokens_hbm, w_hbm, tokens_ref, w_ref, total, token_sems, w_sems, beside, finish
):
    columns = w_ref.shape[1]
    chunks = len(depths)
    parts = [pl.ds(sum(depths[:chunk]), depths[chunk]) for chunk in range(chunks)]
    copies = [
        (
            pltpu.make_async_copy(
                tokens_hbm.at[:, part], tokens_ref.at[:, part], token_sems.at[chunk]
            ),
            pltpu.make_async_copy(w_hbm.at[part], w_ref.at[part], w_sems.at[chunk]),
        )
        for chunk, part in enumerate(parts)
    ]
    for pair in copies[:WINDOW]:
        for copy in pair:
            copy.start()
    for chunk, (part, pair) in enumerate(zip(parts, copies)):
        for copy in pair:
            copy.wait()
        if chunk + WINDOW < chunks:
            for copy in copies[chunk + WINDOW]:
                copy.start()
        if chunk == 1:
            beside()
        if chunk < chunks - 1:
            product = jnp.dot(
                tokens_ref[:, part], w_ref[part], preferred_element_type=jnp.float32
            )
            total[...] = product if chunk == 0 else total[...] + product
            continue
        for block in range(columns // BLOCK):
            cols = pl.ds(block * BLOCK, BLOCK)
            product = total[:, cols] + jnp.dot(
                tokens_ref[:, part], w_ref[part, cols], preferred_element_type=jnp.float32
            )
            for head in range(BLOCK // HEAD_DIM):
                finish(
                    block * BLOCK + head * HEAD_DIM,
                    product[:, head * HEAD_DIM : (head + 1) * HEAD_DIM],
                )


def keyval_kernel(
    depths, pos_hbm, within_hbm, starts_hbm, tokens_hbm, w_hbm, out_ref, turn_hbm, tokens_ref,
    w_ref, total, turn_ref, turn_sem, token_sems, w_sems, pos_ref, within_ref, starts_ref, table_sems
):
    tables = [
        pltpu.make_async_copy(pos_hbm, pos_ref, table_sems.at[0]),
        pltpu.make_async_copy(within_hbm, within_ref, table_sems.at[1]),
        pltpu.make_async_copy(starts_hbm, starts_ref, table_sems.at[2]),
    ]
    for copy in tables:
        copy.start()
    turn_copy = pltpu.make_async_copy(
        turn_ref, turn_hbm.at[pl.ds(0, turn_ref.shape[0])], turn_sem
    )

    def beside():
        for copy in tables:
            copy.wait()
        for run in range(out_ref.shape[0] // SPAN):
            turn_ref[pl.ds(run * SPAN, SPAN)] = run_rotation(
                within_ref, starts_ref, own_run(pos_ref, run)
            )
        turn_copy.start()

    def finish(place, piece):
        if place < HEAD_DIM:
            piece = rotate(piece, *spread(turn_ref[...]))
        out_ref[:, place : place + HEAD_DIM] = piece.astype(out_ref.dtype)

    accumulate(
        depths, tokens_hbm, w_hbm, tokens_ref, w_ref, total, token_sems, w_sems, beside, finish
    )
    turn_copy.wait()


def query_kernel(
    depths, turn_hbm, tokens_hbm, w_hbm, out_ref, tokens_ref, w_ref, total, turn_ref, turn_sem,
    token_sems, w_sems
):
    turn_copy = pltpu.make_async_copy(
        turn_hbm.at[pl.ds(0, turn_ref.shape[0])], turn_ref, turn_sem
    )
    turn_copy.start()

    def finish(place, piece):
        piece = rotate(piece, *spread(turn_ref[...]))
        out_ref[:, place : place + HEAD_DIM] = piece.astype(out_ref.dtype)

    accumulate(
        depths, tokens_hbm, w_hbm, tokens_ref, w_ref, total, token_sems, w_sems, turn_copy.wait,
        finish,
    )


def project(kernel, depths, others, tokens, weights, more_out, more_scratch, limit):
    rows, width = tokens.shape
    columns = weights.shape[1]
    vmem = pl.BlockSpec(memory_space=pltpu.VMEM)
    hbm = pl.BlockSpec(memory_space=pltpu.HBM)
    return pl.pallas_call(
        functools.partial(kernel, depths),
        in_specs=[hbm] * (len(others) + 2),
        out_specs=[vmem] + [hbm] * len(more_out),
        out_shape=[jax.ShapeDtypeStruct((rows, columns), jnp.bfloat16)] + more_out,
        scratch_shapes=[
            pltpu.VMEM(tokens.shape, tokens.dtype),
            pltpu.VMEM(weights.shape, weights.dtype),
            pltpu.VMEM((rows, columns), jnp.float32),
            pltpu.VMEM((rows, HEAD_DIM), jnp.float32),
            pltpu.SemaphoreType.DMA,
            pltpu.SemaphoreType.DMA((len(depths),)),
            pltpu.SemaphoreType.DMA((len(depths),)),
        ]
        + more_scratch,
        compiler_params=pltpu.CompilerParams(vmem_limit_bytes=limit * MIB),
        cost_estimate=pl.CostEstimate(
            flops=2 * rows * width * columns,
            bytes_accessed=2 * (rows * width + width * columns),
            transcendentals=0,
        ),
    )(*others, tokens, weights)


def keyval(tokens, w_keyval, positions):
    within, starts = rotation_tables(positions.shape[0] // SPAN)
    return project(
        keyval_kernel,
        (DEPTH,) * (tokens.shape[1] // DEPTH),
        [positions, within, starts],
        tokens,
        w_keyval,
        [jax.ShapeDtypeStruct((tokens.shape[0] * 64, HEAD_DIM), jnp.float32)],
        [
            pltpu.SMEM(positions.shape, positions.dtype),
            pltpu.VMEM(within.shape, within.dtype),
            pltpu.VMEM(starts.shape, starts.dtype),
            pltpu.SemaphoreType.DMA((3,)),
        ],
        58,
    )


def attention_kernel(masks, last, pos_ref, q_ref, kv_ref, *refs):
    if last:
        _, _, out_ref, top_ref, total_ref, order = refs
    else:
        top_ref, total_ref, order = refs
    heads = q_ref.shape[1] // HEAD_DIM
    me = lax.axis_index("outer") * lax.axis_size("inner") + lax.axis_index("inner")
    packs = heads // PACK
    causal = lax.broadcasted_iota(jnp.int32, (SPAN, SPAN), 1) <= lax.broadcasted_iota(
        jnp.int32, (SPAN, SPAN), 0
    )
    causal = jnp.concatenate([causal] * PACK, 0)
    ones = jnp.ones((SPAN, HEAD_DIM), jnp.bfloat16)

    def visit(part, slots, first):
        rows = pl.ds(pl.multiple_of(part * SPAN, SPAN), SPAN)
        starts = [pl.multiple_of(slot * SPAN, SPAN) for slot in slots]
        keys = [kv_ref[pl.ds(start, SPAN), :HEAD_DIM] for start in starts]
        values = jnp.concatenate(
            [
                jnp.concatenate([kv_ref[pl.ds(start, SPAN), HEAD_DIM:], ones], 1)
                for start in starts
            ],
            0,
        )

        def score(pack):
            queries = jnp.concatenate(
                [
                    q_ref[rows, head * HEAD_DIM : (head + 1) * HEAD_DIM]
                    for head in range(pack * PACK, (pack + 1) * PACK)
                ],
                0,
            )
            return [
                lax.dot_general(
                    queries, key, (((1,), (1,)), ((), ())), preferred_element_type=jnp.float32
                )
                for key in keys
            ]

        def weigh(pack, scores):
            if first:
                scores[0] = jnp.where(causal, scores[0], NEG_FILL)
            best = jnp.max(functools.reduce(jnp.maximum, scores), axis=1, keepdims=True)
            if first:
                top, factor = jnp.broadcast_to(best, (PACK * SPAN, HEAD_DIM)), None
            else:
                before = top_ref[part, pack]
                top = jnp.maximum(before, best)
                factor = jnp.exp2((before - top) * LOG2_SCALE)
            top_ref[part, pack] = top
            wide = jnp.concatenate([top, top], 1)
            weights = [
                jnp.exp2((piece - wide) * LOG2_SCALE).astype(jnp.bfloat16) for piece in scores
            ]
            return jnp.concatenate(weights, 1), factor

        def add(pack, weights, factor):
            added = jnp.dot(weights, values, preferred_element_type=jnp.float32)
            if first:
                total_ref[part, pack] = added
            else:
                total_ref[part, pack] = (
                    total_ref[part, pack] * jnp.concatenate([factor, factor], 1) + added
                )

        scores = [score(pack) for pack in range(AHEAD)]
        weighed = None
        for pack in range(packs):
            if pack + AHEAD < packs:
                scores.append(score(pack + AHEAD))
            following = weigh(pack, scores[pack])
            if pack:
                add(pack - 1, *weighed)
            weighed = following
        add(packs - 1, *weighed)

    def one_run(part, carry):
        own = own_run(pos_ref, part)
        count = jnp.int32(0)
        for place, mask in enumerate(masks):
            for half in range(2):
                block = pos_ref[(me ^ mask) * (2 * SPAN) + half * SPAN] // SPAN
                order[count] = place * 2 + half
                count = count + (block < own).astype(jnp.int32)
        odd = count % GROUP
        for extra in range(last, GROUP):

            @pl.when(odd == extra)
            def _():
                slots = [order[place] for place in range(extra)]
                visit(part, slots if last else [part] + slots, not last)

        def several(step, carry):
            visit(part, [order[odd + GROUP * step + place] for place in range(GROUP)], False)
            return carry

        lax.fori_loop(0, count // GROUP, several, 0)
        if last:
            rows = pl.ds(pl.multiple_of(part * SPAN, SPAN), SPAN)
            for head in range(heads):
                start = head % PACK * SPAN
                sums = total_ref[part, head // PACK, start : start + SPAN]
                out_ref[rows, head * HEAD_DIM : (head + 1) * HEAD_DIM] = (
                    sums[:, :HEAD_DIM] / sums[:, HEAD_DIM:]
                ).astype(out_ref.dtype)
        return carry

    lax.fori_loop(0, q_ref.shape[0] // SPAN, one_run, 0)


def attend(queries, pieces, positions, masks, state=()):
    last = bool(state)
    heads = queries.shape[1] // HEAD_DIM
    runs = queries.shape[0] // SPAN
    vmem = pl.BlockSpec(memory_space=pltpu.VMEM)
    smem = pl.BlockSpec(memory_space=pltpu.SMEM)
    shapes = [
        jax.ShapeDtypeStruct((runs, heads // PACK, PACK * SPAN, HEAD_DIM), jnp.float32),
        jax.ShapeDtypeStruct((runs, heads // PACK, PACK * SPAN, 2 * HEAD_DIM), jnp.float32),
    ]
    aliases = {}
    if last:
        shapes = [jax.ShapeDtypeStruct(queries.shape, jnp.bfloat16)] + shapes
        aliases = {3: 1, 4: 2}
    return pl.pallas_call(
        functools.partial(attention_kernel, masks, last),
        in_specs=[smem, vmem, vmem] + [vmem] * len(state),
        out_specs=[vmem] * len(shapes),
        out_shape=shapes,
        input_output_aliases=aliases,
        scratch_shapes=[pltpu.SMEM((2 * len(masks) + 1,), jnp.int32)],
        compiler_params=pltpu.CompilerParams(vmem_limit_bytes=24 * MIB),
    )(positions, queries, pieces, *state)


def exchanged(value, mask):
    count = lax.axis_size("outer") * lax.axis_size("inner")
    return lax.ppermute(value, SEQ_AXES, [(source, source ^ mask) for source in range(count)])


def body(tokens, positions, w_query, w_keyval):
    count = lax.axis_size("outer") * lax.axis_size("inner")
    masks = list(range(0, count, 2))
    stacked, turn = keyval(tokens, w_keyval, positions)
    direct = [stacked] + [exchanged(stacked, mask) for mask in masks[1:]]
    depths = (DEPTH,) * (tokens.shape[1] // DEPTH)
    queries = project(query_kernel, depths, [turn], tokens, w_query, [], [], 52)[0]
    queries, *direct = lax.optimization_barrier([queries, *direct])
    direct = jnp.concatenate(direct, 0)
    relayed = exchanged(direct, 1)
    state = attend(queries, direct, positions, masks)
    return attend(queries, relayed, positions, [mask ^ 1 for mask in masks], state)[0]


def solution(mesh):
    placed = (P(SEQ_AXES, None), P(), P(None, "head"), P(None, "head"))
    return jax.shard_map(
        body, mesh=mesh, in_specs=placed, out_specs=P(SEQ_AXES, "head"), check_vma=False
    )
```

```python
import functools
import math

import jax
import jax.numpy as jnp
import numpy as np
from jax import lax
from jax.experimental import pallas as pl
from jax.experimental.pallas import tpu as pltpu
from jax.sharding import PartitionSpec as P

HEAD_DIM = 128
HALF = HEAD_DIM // 2
SPAN = 256
ROPE_BASE = 500000.0
NEG_FILL = -1e30
LOG2_SCALE = math.log2(math.e) / math.sqrt(HEAD_DIM)
MIB = 1024 * 1024
BLOCK = 256
DEPTH = 1024
WINDOW = 3
GROUP = 4
AHEAD = 1
PACK = 4
SEQ_AXES = ("outer", "inner")


def rotation_tables(runs):
    freqs = ROPE_BASE ** (-(np.arange(HALF, dtype=np.float64) * 2.0) / HEAD_DIM)
    freqs = np.concatenate([freqs, freqs])
    within = np.arange(SPAN, dtype=np.float64)[:, None] * freqs
    starts = (np.arange(runs, dtype=np.float64) * SPAN)[:, None] * freqs
    within = np.stack([np.cos(within), np.sin(within)]).astype(np.float32)
    starts = np.stack([np.cos(starts), np.sin(starts)], 1).astype(np.float32)
    return jnp.asarray(within), jnp.asarray(starts)


def run_rotation(within_ref, starts_ref, run):
    cos_in, sin_in = within_ref[0], within_ref[1]
    start = starts_ref[run]
    cos_at, sin_at = start[0:1], start[1:2]
    lane = lax.broadcasted_iota(jnp.int32, (SPAN, HEAD_DIM), 1)
    cosine = cos_in * cos_at - sin_in * sin_at
    sine = sin_in * cos_at + cos_in * sin_at
    return jnp.where(lane < HALF, cosine, sine)


def spread(turn):
    lane = lax.broadcasted_iota(jnp.int32, turn.shape, 1)
    other = pltpu.roll(turn, HALF, 1)
    return jnp.where(lane < HALF, turn, other), jnp.where(lane < HALF, -other, turn)


def rotate(rows, cosine, sine):
    return rows * cosine + pltpu.roll(rows, HALF, 1) * sine


def own_start(pos_ref, index):
    row = lax.axis_index("outer") * lax.axis_size("inner") + lax.axis_index("inner")
    return pos_ref[row * (2 * SPAN) + index * SPAN]


def accumulate(
    depths, tokens_hbm, w_hbm, tokens_ref, w_ref, total, token_sems, w_sems, beside, finish
):
    columns = w_ref.shape[1]
    chunks = len(depths)
    parts = [pl.ds(sum(depths[:chunk]), depths[chunk]) for chunk in range(chunks)]
    copies = [
        (
            pltpu.make_async_copy(
                tokens_hbm.at[:, part], tokens_ref.at[:, part], token_sems.at[chunk]
            ),
            pltpu.make_async_copy(w_hbm.at[part], w_ref.at[part], w_sems.at[chunk]),
        )
        for chunk, part in enumerate(parts)
    ]
    for pair in copies[:WINDOW]:
        for copy in pair:
            copy.start()
    for chunk, (part, pair) in enumerate(zip(parts, copies)):
        for copy in pair:
            copy.wait()
        if chunk + WINDOW < chunks:
            for copy in copies[chunk + WINDOW]:
                copy.start()
        if chunk == 1:
            beside()
        if chunk < chunks - 1:
            product = jnp.dot(
                tokens_ref[:, part], w_ref[part], preferred_element_type=jnp.float32
            )
            total[...] = product if chunk == 0 else total[...] + product
            continue
        for block in range(columns // BLOCK):
            cols = pl.ds(block * BLOCK, BLOCK)
            product = total[:, cols] + jnp.dot(
                tokens_ref[:, part], w_ref[part, cols], preferred_element_type=jnp.float32
            )
            for head in range(BLOCK // HEAD_DIM):
                finish(
                    block * BLOCK + head * HEAD_DIM,
                    product[:, head * HEAD_DIM : (head + 1) * HEAD_DIM],
                )


def keyval_kernel(
    depths, pos_hbm, within_hbm, starts_hbm, tokens_hbm, w_hbm, out_ref, turn_hbm, tokens_ref,
    w_ref, total, turn_ref, turn_sem, token_sems, w_sems, pos_ref, within_ref, starts_ref, table_sems
):
    tables = [
        pltpu.make_async_copy(pos_hbm, pos_ref, table_sems.at[0]),
        pltpu.make_async_copy(within_hbm, within_ref, table_sems.at[1]),
        pltpu.make_async_copy(starts_hbm, starts_ref, table_sems.at[2]),
    ]
    for copy in tables:
        copy.start()
    turn_copy = pltpu.make_async_copy(
        turn_ref, turn_hbm.at[pl.ds(0, turn_ref.shape[0])], turn_sem
    )

    def beside():
        for copy in tables:
            copy.wait()
        for run in range(out_ref.shape[0] // SPAN):
            turn_ref[pl.ds(run * SPAN, SPAN)] = run_rotation(
                within_ref, starts_ref, lax.div(own_start(pos_ref, run), SPAN)
            )
        turn_copy.start()

    def finish(place, piece):
        if place < HEAD_DIM:
            piece = rotate(piece, *spread(turn_ref[...]))
        out_ref[:, place : place + HEAD_DIM] = piece.astype(out_ref.dtype)

    accumulate(
        depths, tokens_hbm, w_hbm, tokens_ref, w_ref, total, token_sems, w_sems, beside, finish
    )
    turn_copy.wait()


def query_kernel(
    depths, turn_hbm, tokens_hbm, w_hbm, out_ref, tokens_ref, w_ref, total, turn_ref, turn_sem,
    token_sems, w_sems
):
    turn_copy = pltpu.make_async_copy(
        turn_hbm.at[pl.ds(0, turn_ref.shape[0])], turn_ref, turn_sem
    )
    turn_copy.start()

    def finish(place, piece):
        piece = rotate(piece, *spread(turn_ref[...]))
        out_ref[:, place : place + HEAD_DIM] = piece.astype(out_ref.dtype)

    accumulate(
        depths, tokens_hbm, w_hbm, tokens_ref, w_ref, total, token_sems, w_sems, turn_copy.wait,
        finish,
    )


def project(kernel, depths, others, tokens, weights, more_out, more_scratch, limit):
    rows, width = tokens.shape
    columns = weights.shape[1]
    vmem = pl.BlockSpec(memory_space=pltpu.VMEM)
    hbm = pl.BlockSpec(memory_space=pltpu.HBM)
    return pl.pallas_call(
        functools.partial(kernel, depths),
        in_specs=[hbm] * (len(others) + 2),
        out_specs=[vmem] + [hbm] * len(more_out),
        out_shape=[jax.ShapeDtypeStruct((rows, columns), jnp.bfloat16)] + more_out,
        scratch_shapes=[
            pltpu.VMEM(tokens.shape, tokens.dtype),
            pltpu.VMEM(weights.shape, weights.dtype),
            pltpu.VMEM((rows, columns), jnp.float32),
            pltpu.VMEM((rows, HEAD_DIM), jnp.float32),
            pltpu.SemaphoreType.DMA,
            pltpu.SemaphoreType.DMA((len(depths),)),
            pltpu.SemaphoreType.DMA((len(depths),)),
        ]
        + more_scratch,
        compiler_params=pltpu.CompilerParams(vmem_limit_bytes=limit * MIB),
        cost_estimate=pl.CostEstimate(
            flops=2 * rows * width * columns,
            bytes_accessed=2 * (rows * width + width * columns),
            transcendentals=0,
        ),
    )(*others, tokens, weights)


def keyval(tokens, w_keyval, positions):
    within, starts = rotation_tables(positions.shape[0] // SPAN)
    return project(
        keyval_kernel,
        (DEPTH,) * (tokens.shape[1] // DEPTH),
        [positions, within, starts],
        tokens,
        w_keyval,
        [jax.ShapeDtypeStruct((tokens.shape[0] * 64, HEAD_DIM), jnp.float32)],
        [
            pltpu.SMEM(positions.shape, positions.dtype),
            pltpu.VMEM(within.shape, within.dtype),
            pltpu.VMEM(starts.shape, starts.dtype),
            pltpu.SemaphoreType.DMA((3,)),
        ],
        58,
    )


def attention_kernel(masks, last, pos_ref, q_ref, kv_ref, *refs):
    if last:
        _, _, out_ref, top_ref, total_ref, order = refs
    else:
        top_ref, total_ref, order = refs
    heads = q_ref.shape[1] // HEAD_DIM
    me = lax.axis_index("outer") * lax.axis_size("inner") + lax.axis_index("inner")
    packs = heads // PACK
    causal = lax.broadcasted_iota(jnp.int32, (SPAN, SPAN), 1) <= lax.broadcasted_iota(
        jnp.int32, (SPAN, SPAN), 0
    )
    causal = jnp.concatenate([causal] * PACK, 0)
    ones = jnp.ones((SPAN, HEAD_DIM), jnp.bfloat16)

    def visit(part, slots, first):
        rows = pl.ds(pl.multiple_of(part * SPAN, SPAN), SPAN)
        starts = [pl.multiple_of(slot * SPAN, SPAN) for slot in slots]
        keys = [kv_ref[pl.ds(start, SPAN), :HEAD_DIM] for start in starts]
        values = jnp.concatenate(
            [
                jnp.concatenate([kv_ref[pl.ds(start, SPAN), HEAD_DIM:], ones], 1)
                for start in starts
            ],
            0,
        )

        def score(pack):
            queries = jnp.concatenate(
                [
                    q_ref[rows, head * HEAD_DIM : (head + 1) * HEAD_DIM]
                    for head in range(pack * PACK, (pack + 1) * PACK)
                ],
                0,
            )
            return [
                lax.dot_general(
                    queries, key, (((1,), (1,)), ((), ())), preferred_element_type=jnp.float32
                )
                for key in keys
            ]

        def weigh(pack, scores):
            if first:
                scores[0] = jnp.where(causal, scores[0], NEG_FILL)
            best = jnp.max(functools.reduce(jnp.maximum, scores), axis=1, keepdims=True)
            if first:
                top, factor = jnp.broadcast_to(best, (PACK * SPAN, HEAD_DIM)), None
            else:
                before = top_ref[part, pack]
                top = jnp.maximum(before, best)
                factor = jnp.exp2((before - top) * LOG2_SCALE)
            top_ref[part, pack] = top
            wide = jnp.concatenate([top, top], 1)
            weights = [
                jnp.exp2((piece - wide) * LOG2_SCALE).astype(jnp.bfloat16) for piece in scores
            ]
            return jnp.concatenate(weights, 1), factor

        def add(pack, weights, factor):
            added = jnp.dot(weights, values, preferred_element_type=jnp.float32)
            if first:
                total_ref[part, pack] = added
            else:
                total_ref[part, pack] = (
                    total_ref[part, pack] * jnp.concatenate([factor, factor], 1) + added
                )

        scores = [score(pack) for pack in range(AHEAD)]
        weighed = None
        for pack in range(packs):
            if pack + AHEAD < packs:
                scores.append(score(pack + AHEAD))
            following = weigh(pack, scores[pack])
            if pack:
                add(pack - 1, *weighed)
            weighed = following
        add(packs - 1, *weighed)

    def one_run(part, carry):
        own = own_start(pos_ref, part)
        count = jnp.int32(0)
        for place, mask in enumerate(masks):
            for half in range(2):
                start = pos_ref[(me ^ mask) * (2 * SPAN) + half * SPAN]
                order[count] = place * 2 + half
                count = count + (start < own).astype(jnp.int32)
        odd = lax.rem(count, GROUP)
        for extra in range(last, GROUP):

            @pl.when(odd == extra)
            def _():
                slots = [order[place] for place in range(extra)]
                visit(part, slots if last else [part] + slots, not last)

        def several(step, carry):
            visit(part, [order[odd + GROUP * step + place] for place in range(GROUP)], False)
            return carry

        lax.fori_loop(0, lax.div(count, GROUP), several, 0)
        if last:
            rows = pl.ds(pl.multiple_of(part * SPAN, SPAN), SPAN)
            for head in range(heads):
                start = head % PACK * SPAN
                sums = total_ref[part, head // PACK, start : start + SPAN]
                out_ref[rows, head * HEAD_DIM : (head + 1) * HEAD_DIM] = (
                    sums[:, :HEAD_DIM] / sums[:, HEAD_DIM:]
                ).astype(out_ref.dtype)
        return carry

    lax.fori_loop(0, q_ref.shape[0] // SPAN, one_run, 0)


def attend(queries, pieces, positions, masks, state=()):
    last = bool(state)
    heads = queries.shape[1] // HEAD_DIM
    runs = queries.shape[0] // SPAN
    vmem = pl.BlockSpec(memory_space=pltpu.VMEM)
    smem = pl.BlockSpec(memory_space=pltpu.SMEM)
    shapes = [
        jax.ShapeDtypeStruct((runs, heads // PACK, PACK * SPAN, HEAD_DIM), jnp.float32),
        jax.ShapeDtypeStruct((runs, heads // PACK, PACK * SPAN, 2 * HEAD_DIM), jnp.float32),
    ]
    aliases = {}
    if last:
        shapes = [jax.ShapeDtypeStruct(queries.shape, jnp.bfloat16)] + shapes
        aliases = {3: 1, 4: 2}
    return pl.pallas_call(
        functools.partial(attention_kernel, masks, last),
        in_specs=[smem, vmem, vmem] + [vmem] * len(state),
        out_specs=[vmem] * len(shapes),
        out_shape=shapes,
        input_output_aliases=aliases,
        scratch_shapes=[pltpu.SMEM((2 * len(masks) + 1,), jnp.int32)],
        compiler_params=pltpu.CompilerParams(vmem_limit_bytes=24 * MIB),
    )(positions, queries, pieces, *state)


def exchanged(value, mask):
    count = lax.axis_size("outer") * lax.axis_size("inner")
    return lax.ppermute(value, SEQ_AXES, [(source, source ^ mask) for source in range(count)])


def body(tokens, positions, w_query, w_keyval):
    count = lax.axis_size("outer") * lax.axis_size("inner")
    masks = list(range(0, count, 2))
    stacked, turn = keyval(tokens, w_keyval, positions)
    direct = [stacked] + [exchanged(stacked, mask) for mask in masks[1:]]
    depths = (DEPTH,) * (tokens.shape[1] // DEPTH)
    queries = project(query_kernel, depths, [turn], tokens, w_query, [], [], 52)[0]
    queries, *direct = lax.optimization_barrier([queries, *direct])
    direct = jnp.concatenate(direct, 0)
    relayed = exchanged(direct, 1)
    state = attend(queries, direct, positions, masks)
    return attend(queries, relayed, positions, [mask ^ 1 for mask in masks], state)[0]


def solution(mesh):
    placed = (P(SEQ_AXES, None), P(), P(None, "head"), P(None, "head"))
    return jax.shard_map(
        body, mesh=mesh, in_specs=placed, out_specs=P(SEQ_AXES, "head"), check_vma=False
    )
```

```python
import functools
import math

import jax
import jax.numpy as jnp
import numpy as np
from jax import lax
from jax.experimental import pallas as pl
from jax.experimental.pallas import tpu as pltpu
from jax.sharding import PartitionSpec as P

HEAD_DIM = 128
HALF = HEAD_DIM // 2
SPAN = 256
ROPE_BASE = 500000.0
NEG_FILL = -1e30
LOG2_SCALE = math.log2(math.e) / math.sqrt(HEAD_DIM)
MIB = 1024 * 1024
BLOCK = 256
DEPTH = 1024
WINDOW = 3
GROUP = 5
AHEAD = 1
PACK = 4
SEQ_AXES = ("outer", "inner")


def rotation_tables(runs):
    freqs = ROPE_BASE ** (-(np.arange(HALF, dtype=np.float64) * 2.0) / HEAD_DIM)
    freqs = np.concatenate([freqs, freqs])
    within = np.arange(SPAN, dtype=np.float64)[:, None] * freqs
    starts = (np.arange(runs, dtype=np.float64) * SPAN)[:, None] * freqs
    within = np.stack([np.cos(within), np.sin(within)]).astype(np.float32)
    starts = np.stack([np.cos(starts), np.sin(starts)], 1).astype(np.float32)
    return jnp.asarray(within), jnp.asarray(starts)


def run_rotation(within_ref, starts_ref, run):
    cos_in, sin_in = within_ref[0], within_ref[1]
    start = starts_ref[run]
    cos_at, sin_at = start[0:1], start[1:2]
    lane = lax.broadcasted_iota(jnp.int32, (SPAN, HEAD_DIM), 1)
    cosine = cos_in * cos_at - sin_in * sin_at
    sine = sin_in * cos_at + cos_in * sin_at
    return jnp.where(lane < HALF, cosine, sine)


def spread(turn):
    lane = lax.broadcasted_iota(jnp.int32, turn.shape, 1)
    other = pltpu.roll(turn, HALF, 1)
    return jnp.where(lane < HALF, turn, other), jnp.where(lane < HALF, -other, turn)


def rotate(rows, cosine, sine):
    return rows * cosine + pltpu.roll(rows, HALF, 1) * sine


def own_start(pos_ref, index):
    row = lax.axis_index("outer") * lax.axis_size("inner") + lax.axis_index("inner")
    return pos_ref[row * (2 * SPAN) + index * SPAN]


def accumulate(
    depths, tokens_hbm, w_hbm, tokens_ref, w_ref, total, token_sems, w_sems, beside, finish
):
    columns = w_ref.shape[1]
    chunks = len(depths)
    parts = [pl.ds(sum(depths[:chunk]), depths[chunk]) for chunk in range(chunks)]
    copies = [
        (
            pltpu.make_async_copy(
                tokens_hbm.at[:, part], tokens_ref.at[:, part], token_sems.at[chunk]
            ),
            pltpu.make_async_copy(w_hbm.at[part], w_ref.at[part], w_sems.at[chunk]),
        )
        for chunk, part in enumerate(parts)
    ]
    for pair in copies[:WINDOW]:
        for copy in pair:
            copy.start()
    for chunk, (part, pair) in enumerate(zip(parts, copies)):
        for copy in pair:
            copy.wait()
        if chunk + WINDOW < chunks:
            for copy in copies[chunk + WINDOW]:
                copy.start()
        if chunk == 1:
            beside()
        if chunk < chunks - 1:
            product = jnp.dot(
                tokens_ref[:, part], w_ref[part], preferred_element_type=jnp.float32
            )
            total[...] = product if chunk == 0 else total[...] + product
            continue
        for block in range(columns // BLOCK):
            cols = pl.ds(block * BLOCK, BLOCK)
            product = total[:, cols] + jnp.dot(
                tokens_ref[:, part], w_ref[part, cols], preferred_element_type=jnp.float32
            )
            for head in range(BLOCK // HEAD_DIM):
                finish(
                    block * BLOCK + head * HEAD_DIM,
                    product[:, head * HEAD_DIM : (head + 1) * HEAD_DIM],
                )


def keyval_kernel(
    depths, pos_hbm, within_hbm, starts_hbm, tokens_hbm, w_hbm, out_ref, turn_hbm, tokens_ref,
    w_ref, total, turn_ref, turn_sem, token_sems, w_sems, pos_ref, within_ref, starts_ref, table_sems
):
    tables = [
        pltpu.make_async_copy(pos_hbm, pos_ref, table_sems.at[0]),
        pltpu.make_async_copy(within_hbm, within_ref, table_sems.at[1]),
        pltpu.make_async_copy(starts_hbm, starts_ref, table_sems.at[2]),
    ]
    for copy in tables:
        copy.start()
    turn_copy = pltpu.make_async_copy(
        turn_ref, turn_hbm.at[pl.ds(0, turn_ref.shape[0])], turn_sem
    )

    def beside():
        for copy in tables:
            copy.wait()
        for run in range(out_ref.shape[0] // SPAN):
            turn_ref[pl.ds(run * SPAN, SPAN)] = run_rotation(
                within_ref, starts_ref, lax.div(own_start(pos_ref, run), SPAN)
            )
        turn_copy.start()

    def finish(place, piece):
        if place < HEAD_DIM:
            piece = rotate(piece, *spread(turn_ref[...]))
        out_ref[:, place : place + HEAD_DIM] = piece.astype(out_ref.dtype)

    accumulate(
        depths, tokens_hbm, w_hbm, tokens_ref, w_ref, total, token_sems, w_sems, beside, finish
    )
    turn_copy.wait()


def query_kernel(
    depths, turn_hbm, tokens_hbm, w_hbm, out_ref, tokens_ref, w_ref, total, turn_ref, turn_sem,
    token_sems, w_sems
):
    turn_copy = pltpu.make_async_copy(
        turn_hbm.at[pl.ds(0, turn_ref.shape[0])], turn_ref, turn_sem
    )
    turn_copy.start()

    def finish(place, piece):
        piece = rotate(piece, *spread(turn_ref[...]))
        out_ref[:, place : place + HEAD_DIM] = piece.astype(out_ref.dtype)

    accumulate(
        depths, tokens_hbm, w_hbm, tokens_ref, w_ref, total, token_sems, w_sems, turn_copy.wait,
        finish,
    )


def project(kernel, depths, others, tokens, weights, more_out, more_scratch, limit):
    rows, width = tokens.shape
    columns = weights.shape[1]
    vmem = pl.BlockSpec(memory_space=pltpu.VMEM)
    hbm = pl.BlockSpec(memory_space=pltpu.HBM)
    return pl.pallas_call(
        functools.partial(kernel, depths),
        in_specs=[hbm] * (len(others) + 2),
        out_specs=[vmem] + [hbm] * len(more_out),
        out_shape=[jax.ShapeDtypeStruct((rows, columns), jnp.bfloat16)] + more_out,
        scratch_shapes=[
            pltpu.VMEM(tokens.shape, tokens.dtype),
            pltpu.VMEM(weights.shape, weights.dtype),
            pltpu.VMEM((rows, columns), jnp.float32),
            pltpu.VMEM((rows, HEAD_DIM), jnp.float32),
            pltpu.SemaphoreType.DMA,
            pltpu.SemaphoreType.DMA((len(depths),)),
            pltpu.SemaphoreType.DMA((len(depths),)),
        ]
        + more_scratch,
        compiler_params=pltpu.CompilerParams(vmem_limit_bytes=limit * MIB),
        cost_estimate=pl.CostEstimate(
            flops=2 * rows * width * columns,
            bytes_accessed=2 * (rows * width + width * columns),
            transcendentals=0,
        ),
    )(*others, tokens, weights)


def keyval(tokens, w_keyval, positions):
    within, starts = rotation_tables(positions.shape[0] // SPAN)
    return project(
        keyval_kernel,
        (DEPTH,) * (tokens.shape[1] // DEPTH),
        [positions, within, starts],
        tokens,
        w_keyval,
        [jax.ShapeDtypeStruct((tokens.shape[0] * 64, HEAD_DIM), jnp.float32)],
        [
            pltpu.SMEM(positions.shape, positions.dtype),
            pltpu.VMEM(within.shape, within.dtype),
            pltpu.VMEM(starts.shape, starts.dtype),
            pltpu.SemaphoreType.DMA((3,)),
        ],
        58,
    )


def attention_kernel(masks, last, pos_ref, q_ref, kv_ref, *refs):
    if last:
        _, _, out_ref, top_ref, total_ref, order = refs
    else:
        top_ref, total_ref, order = refs
    heads = q_ref.shape[1] // HEAD_DIM
    me = lax.axis_index("outer") * lax.axis_size("inner") + lax.axis_index("inner")
    packs = heads // PACK
    causal = lax.broadcasted_iota(jnp.int32, (SPAN, SPAN), 1) <= lax.broadcasted_iota(
        jnp.int32, (SPAN, SPAN), 0
    )
    causal = jnp.concatenate([causal] * PACK, 0)
    ones = jnp.ones((SPAN, HEAD_DIM), jnp.bfloat16)

    def visit(part, slots, first):
        rows = pl.ds(pl.multiple_of(part * SPAN, SPAN), SPAN)
        starts = [pl.multiple_of(slot * SPAN, SPAN) for slot in slots]
        keys = [kv_ref[pl.ds(start, SPAN), :HEAD_DIM] for start in starts]
        values = jnp.concatenate(
            [
                jnp.concatenate([kv_ref[pl.ds(start, SPAN), HEAD_DIM:], ones], 1)
                for start in starts
            ],
            0,
        )

        def score(pack):
            queries = jnp.concatenate(
                [
                    q_ref[rows, head * HEAD_DIM : (head + 1) * HEAD_DIM]
                    for head in range(pack * PACK, (pack + 1) * PACK)
                ],
                0,
            )
            return [
                lax.dot_general(
                    queries, key, (((1,), (1,)), ((), ())), preferred_element_type=jnp.float32
                )
                for key in keys
            ]

        def weigh(pack, scores):
            if first:
                scores[0] = jnp.where(causal, scores[0], NEG_FILL)
            best = jnp.max(functools.reduce(jnp.maximum, scores), axis=1, keepdims=True)
            if first:
                top, factor = jnp.broadcast_to(best, (PACK * SPAN, HEAD_DIM)), None
            else:
                before = top_ref[part, pack]
                top = jnp.maximum(before, best)
                factor = jnp.exp2((before - top) * LOG2_SCALE)
            top_ref[part, pack] = top
            wide = jnp.concatenate([top, top], 1)
            weights = [
                jnp.exp2((piece - wide) * LOG2_SCALE).astype(jnp.bfloat16) for piece in scores
            ]
            return jnp.concatenate(weights, 1), factor

        def add(pack, weights, factor):
            added = jnp.dot(weights, values, preferred_element_type=jnp.float32)
            if first:
                total_ref[part, pack] = added
            else:
                total_ref[part, pack] = (
                    total_ref[part, pack] * jnp.concatenate([factor, factor], 1) + added
                )

        scores = [score(pack) for pack in range(AHEAD)]
        weighed = None
        for pack in range(packs):
            if pack + AHEAD < packs:
                scores.append(score(pack + AHEAD))
            following = weigh(pack, scores[pack])
            if pack:
                add(pack - 1, *weighed)
            weighed = following
        add(packs - 1, *weighed)

    def one_run(part, carry):
        own = own_start(pos_ref, part)
        count = jnp.int32(0)
        for place, mask in enumerate(masks):
            for half in range(2):
                start = pos_ref[(me ^ mask) * (2 * SPAN) + half * SPAN]
                order[count] = place * 2 + half
                count = count + (start < own).astype(jnp.int32)
        odd = lax.rem(count, GROUP)
        for extra in range(last, GROUP):

            @pl.when(odd == extra)
            def _():
                slots = [order[place] for place in range(extra)]
                visit(part, slots if last else [part] + slots, not last)

        def several(step, carry):
            visit(part, [order[odd + GROUP * step + place] for place in range(GROUP)], False)
            return carry

        lax.fori_loop(0, lax.div(count, GROUP), several, 0)
        if last:
            rows = pl.ds(pl.multiple_of(part * SPAN, SPAN), SPAN)
            for head in range(heads):
                start = head % PACK * SPAN
                sums = total_ref[part, head // PACK, start : start + SPAN]
                out_ref[rows, head * HEAD_DIM : (head + 1) * HEAD_DIM] = (
                    sums[:, :HEAD_DIM] / sums[:, HEAD_DIM:]
                ).astype(out_ref.dtype)
        return carry

    lax.fori_loop(0, q_ref.shape[0] // SPAN, one_run, 0)


def attend(queries, pieces, positions, masks, state=()):
    last = bool(state)
    heads = queries.shape[1] // HEAD_DIM
    runs = queries.shape[0] // SPAN
    vmem = pl.BlockSpec(memory_space=pltpu.VMEM)
    smem = pl.BlockSpec(memory_space=pltpu.SMEM)
    shapes = [
        jax.ShapeDtypeStruct((runs, heads // PACK, PACK * SPAN, HEAD_DIM), jnp.float32),
        jax.ShapeDtypeStruct((runs, heads // PACK, PACK * SPAN, 2 * HEAD_DIM), jnp.float32),
    ]
    aliases = {}
    if last:
        shapes = [jax.ShapeDtypeStruct(queries.shape, jnp.bfloat16)] + shapes
        aliases = {3: 1, 4: 2}
    return pl.pallas_call(
        functools.partial(attention_kernel, masks, last),
        in_specs=[smem, vmem, vmem] + [vmem] * len(state),
        out_specs=[vmem] * len(shapes),
        out_shape=shapes,
        input_output_aliases=aliases,
        scratch_shapes=[pltpu.SMEM((2 * len(masks) + 1,), jnp.int32)],
        compiler_params=pltpu.CompilerParams(vmem_limit_bytes=24 * MIB),
    )(positions, queries, pieces, *state)


def exchanged(value, mask):
    count = lax.axis_size("outer") * lax.axis_size("inner")
    return lax.ppermute(value, SEQ_AXES, [(source, source ^ mask) for source in range(count)])


def body(tokens, positions, w_query, w_keyval):
    count = lax.axis_size("outer") * lax.axis_size("inner")
    masks = list(range(0, count, 2))
    stacked, turn = keyval(tokens, w_keyval, positions)
    direct = [stacked] + [exchanged(stacked, mask) for mask in masks[1:]]
    depths = (DEPTH,) * (tokens.shape[1] // DEPTH)
    queries = project(query_kernel, depths, [turn], tokens, w_query, [], [], 52)[0]
    queries, *direct = lax.optimization_barrier([queries, *direct])
    direct = jnp.concatenate(direct, 0)
    relayed = exchanged(direct, 1)
    state = attend(queries, direct, positions, masks)
    return attend(queries, relayed, positions, [mask ^ 1 for mask in masks], state)[0]


def solution(mesh):
    placed = (P(SEQ_AXES, None), P(), P(None, "head"), P(None, "head"))
    return jax.shard_map(
        body, mesh=mesh, in_specs=placed, out_specs=P(SEQ_AXES, "head"), check_vma=False
    )
```
